32 devices in a mesh: row: 8 (over z, x), mp: 4 (over y, core).
Axes of the slice: x: 2, y: 2, z: 4, core: 2. Of those that a mesh axis runs over, the one named last changes fastest.
Arguments:
- token_ids: int32 [64, 128], P('row'), may hold values from 0 to 511
- set_lengths: int32 [64], P('row'), may hold values from 32 to 128
- live_counts: int32 [8], replicated, may hold values from 1 to 8, 32 in all
- embed_table: bfloat16 [512, 5120], replicated, may hold values from -3 to 3
- position_table: bfloat16 [128, 5120], replicated, may hold values from -3 to 3
- norm_gain: float32 [5120], replicated, may hold values from 0.1 to 1.9
- w_query: bfloat16 [5120, 5120], P('row', 'mp')
- w_key: bfloat16 [5120, 5120], P('row', 'mp')
- w_value: bfloat16 [5120, 5120], P('row', 'mp'), may hold values from -0.078125 to 0.078125
- w_out: bfloat16 [5120, 5120], P('mp', 'row'), may hold values from -0.078125 to 0.078125
Outputs:
- verified: bfloat16 [64, 128, 5120], P('row', None, 'mp')
The draws below stay inside these ranges and needn't reach their ends.
Inputs may be any that keep to these rules, and one draw needn't show every extreme that they name: Owner group g has live_counts[g] live sets, its first slots; the counts sum to 32 and one group holds 8. `set_lengths`: positions at or past a set's length are padding.
All inputs are finite; a program needn't handle non-finite values.
Results may differ from the reference program's by a relative error of at most 0.017.
Values may be sent and summed in bfloat16 or wider, within the bound.
A program may use at most 128 MiB of HBM per device.

```python
import math
import jax
import jax.numpy as jnp
import numpy as np
from jax import lax

D = 5120
DH = 128
VOCAB = 512
SEQ = 128
SLOTS = 8
GROUPS = 8
SETS = 64
N_MP = 4


def shared_base(key):
    raw = jax.random.normal(jax.random.fold_in(key, 101), (D, D), jnp.float32)
    return jnp.clip(raw, -4.0, 4.0) * D ** (-0.5)


def draw_w_query(key, part):
    return shared_base(key).astype(jnp.bfloat16)


def draw_w_key(key, part):
    fresh = jnp.clip(jax.random.normal(jax.random.fold_in(key, 202), (D, D), jnp.float32), -4.0, 4.0) * D ** (-0.5)
    mixed_weight = fresh
    return mixed_weight.astype(jnp.bfloat16)


def place_ends(drawn, own_key, low, largest):
    shape = drawn.shape
    place = [jax.random.randint(jax.random.fold_in(own_key, axis), (), 0, shape[axis]) for axis in range(len(shape))]
    drawn = drawn.at[tuple(place)].set(low)
    longest = shape.index(max(shape))
    place[longest] = (place[longest] + 1) % shape[longest]
    return drawn.at[tuple(place)].set(largest)


def levels(key, shape, cuts, smallest, top_value):
    def one(position, shards_of):
        draws = jax.random.uniform(jax.random.fold_in(jax.random.fold_in(key, 6), position), (shards_of,), jnp.float32, smallest / len(cuts), top_value / len(cuts))
        return jnp.repeat(jnp.exp(draws), shape[position] // shards_of).reshape((-1,) + (1,) * (len(shape) - position - 1))

    gain = one(*cuts[0])
    for cut in cuts[1:]:
        gain = gain * one(*cut)
    return gain


def cumulative_ranks(amount, lean):
    loads = [(1 << 20) // math.isqrt(standing ** lean) + 1 for standing in range(1, amount + 1)]
    scale = 1 + sum(loads) // (1 << 30)
    return np.cumsum(np.array([max(1, weight // scale) for weight in loads]))


def skewed_ids(rng, dims, count, slope):
    grid = cumulative_ranks(count, slope)
    lot = jax.random.randint(jax.random.fold_in(rng, 1), dims, 0, int(grid[count - 1]))
    standing = jnp.searchsorted(jnp.asarray(grid, jnp.int32), lot, side="right")
    return jax.random.permutation(jax.random.fold_in(rng, 2), count)[standing].astype(jnp.int32)


def split_up(number_of, total, reach, skew):
    loads = [(1 << 20) // math.isqrt(grade ** skew) + 1 for grade in range(2, number_of + 1)]
    surplus, counts = total - reach - (number_of - 1), [1] * (number_of - 1)
    while surplus > 0:
        candidates = [i for i in range(number_of - 1) if counts[i] < reach]
        mass, budget = sum([loads[i] for i in candidates]), surplus
        for i in candidates:
            more = min(reach - counts[i], max(1, budget * loads[i] // mass), surplus)
            counts[i] = counts[i] + more
            surplus = surplus - more
    return np.array([reach] + counts)


def ragged_sizes(own_key, amount, total, bound, slope):
    if amount == 2:
        one = jax.random.randint(own_key, (), max(1, total - bound), min(bound, total - 1) + 1)
        return jnp.stack([one, total - one])
    sizes = jnp.asarray(split_up(amount, total, bound, slope), jnp.int32)
    twos = (amount - 1) // 2
    giver, sink = sizes[1:1 + 2 * twos:2], sizes[2:2 + 2 * twos:2]
    slack = jnp.minimum(giver - 1, bound - sink)
    passed = jax.random.randint(jax.random.fold_in(own_key, 1), (twos,), 0, 1 << 20) % (slack + 1)
    sizes = sizes.at[1:1 + 2 * twos:2].set(giver - passed).at[2:2 + 2 * twos:2].set(sink + passed)
    return sizes[jax.random.permutation(jax.random.fold_in(own_key, 2), amount)]


def noise(key, shape, spread, reach, cuts=(), held_as=jnp.bfloat16):
    result = jax.random.normal(key, shape, jnp.float32) * spread
    if len(cuts) > 0:
        result = levels(key, shape, cuts, -0.22, 0.18) * result
    return jnp.clip(result, min=-reach, max=reach).astype(held_as)


def setup_inputs(seed: int = 0) -> dict:
    arg_keys = jax.random.split(jax.random.key(seed), 11)
    return {
        "token_ids": place_ends(skewed_ids(arg_keys[0], (SETS, SEQ), VOCAB, 2), jax.random.fold_in(arg_keys[0], 3), 0, VOCAB - 1).astype(jnp.int32),
        "set_lengths": place_ends(jax.random.randint(arg_keys[1], (SETS,), SEQ // 4, SEQ + 1), jax.random.fold_in(arg_keys[1], 1), SEQ // 4, SEQ).astype(jnp.int32),
        "live_counts": ragged_sizes(arg_keys[2], GROUPS, GROUPS * SLOTS // 2, SLOTS, 2).astype(jnp.int32),
        "embed_table": noise(arg_keys[3], (VOCAB, D), 0.5, 3.0),
        "position_table": noise(arg_keys[4], (SEQ, D), 0.5, 3.0),
        "norm_gain": jnp.clip(1.0 + 0.18 * jax.random.normal(arg_keys[5], (D,), jnp.float32), 0.1, 1.9),
        "w_query": draw_w_query(jax.random.fold_in(arg_keys[10], 71), 0),
        "w_key": draw_w_key(jax.random.fold_in(arg_keys[10], 71), 0),
        "w_value": noise(arg_keys[8], (D, D), D ** -0.5, 0.078125, ((0, 8), (1, 4))),
        "w_out": noise(arg_keys[9], (D, D), D ** -0.5, 0.078125, ((0, 4), (1, 8))),
    }


def prepare(group_ids, embed_table, position_table, norm_gain):
    summed = jnp.take(embed_table, group_ids, axis=0).astype(jnp.float32) + position_table.astype(jnp.float32)[None]
    stored = lax.optimization_barrier(summed.astype(jnp.bfloat16))
    widened = stored.astype(jnp.float32)
    inverse = lax.rsqrt(lax.optimization_barrier(jnp.mean(widened * widened, axis=-1, keepdims=True)) + 1e-05)
    normed = (widened * inverse * norm_gain).astype(jnp.bfloat16)
    return (stored, normed)

def attend(query, keys, values, group_lengths, head_size):
    set_count = group_lengths.shape[0]
    seq_len = query.shape[0] // set_count
    q_four = query.astype(jnp.float32).reshape(set_count, seq_len, -1, head_size)
    k_four = keys.astype(jnp.float32).reshape(set_count, seq_len, -1, head_size)
    v_four = values.astype(jnp.float32).reshape(set_count, seq_len, -1, head_size)
    scores = jnp.einsum('sqhd,skhd->shqk', q_four, k_four) * head_size ** (-0.5)
    valid = jnp.arange(seq_len)[None, :] < group_lengths[:, None]
    scores = jnp.where(valid[:, None, None, :], scores, -1e+30)
    highest = lax.optimization_barrier(jnp.max(scores, axis=-1, keepdims=True))
    expo = jnp.exp(scores - highest)
    weights = (expo / lax.optimization_barrier(jnp.sum(expo, axis=-1, keepdims=True))).astype(jnp.bfloat16)
    mixed = jnp.einsum('shqk,skhd->sqhd', weights.astype(jnp.float32), v_four)
    return mixed.astype(jnp.bfloat16).reshape(set_count * seq_len, -1)

def reference(token_ids, set_lengths, live_counts, embed_table, position_table, norm_gain, w_query, w_key, w_value, w_out):

    def one_group(block):
        group_ids, group_lengths, group_count = block
        stored, normed = prepare(group_ids, embed_table, position_table, norm_gain)
        flat = normed.reshape(-1, D)
        query = jnp.dot(flat, w_query, preferred_element_type=jnp.float32).astype(jnp.bfloat16)
        keys = jnp.dot(flat, w_key, preferred_element_type=jnp.float32).astype(jnp.bfloat16)
        values = jnp.dot(flat, w_value, preferred_element_type=jnp.float32).astype(jnp.bfloat16)
        mixed = attend(query, keys, values, group_lengths, DH)
        split = mixed.astype(jnp.float32).reshape(-1, N_MP, D // N_MP)
        out_blocks = w_out.astype(jnp.float32).reshape(N_MP, D // N_MP, D)
        partial_value = jnp.einsum('tmk,mkd->tmd', split, out_blocks)
        rounded = lax.optimization_barrier(partial_value.astype(jnp.bfloat16)).astype(jnp.float32)
        total = lax.optimization_barrier(jnp.sum(rounded, axis=1))
        live = jnp.arange(SLOTS) < group_count
        valid = jnp.arange(SEQ)[None, :] < group_lengths[:, None]
        keep = (live[:, None] & valid).reshape(-1, 1).astype(jnp.float32)
        output = ((stored.reshape(-1, D).astype(jnp.float32) + total) * keep).astype(jnp.bfloat16)
        return output.reshape(SLOTS, SEQ, D)
    blocks = (token_ids.reshape(GROUPS, SLOTS, SEQ), set_lengths.reshape(GROUPS, SLOTS), live_counts)
    return lax.map(one_group, blocks).reshape(SETS, SEQ, D)
```

```python
import functools
import jax
import jax.numpy as jnp
from jax import lax
from jax.experimental import pallas as pl
from jax.experimental.pallas import tpu as pltpu
from jax.sharding import PartitionSpec as P

DH = 128


def attend_kernel(heads, vocab, lengths_ref, live_ref, ids_ref, inv_ref, table_ref, out_ref):
    s = pl.program_id(0)
    seq = out_ref.shape[0]
    width = heads * DH
    length = lengths_ref[s]

    @pl.when(live_ref[s] == 0)
    def _():
        out_ref[...] = jnp.zeros_like(out_ref)

    @pl.when(live_ref[s] != 0)
    def _():
        ids = ids_ref[...].reshape(seq, 1)
        cols = lax.broadcasted_iota(jnp.int32, (seq, vocab + seq), 1)
        rows = lax.broadcasted_iota(jnp.int32, (seq, vocab + seq), 0)
        pick = jnp.where((cols == ids) | (cols == rows + vocab), 1.0, 0.0).astype(jnp.bfloat16)
        inv = inv_ref[...].reshape(seq, 1)
        masked = lax.broadcasted_iota(jnp.int32, (seq, seq), 1) >= length


        pieces = {}
        for part in range(3):
            at = 0
            while at < width:
                step = min(2 * DH, width - at)
                got = jnp.dot(
                    pick, table_ref[:, part * width + at:part * width + at + step],
                    preferred_element_type=jnp.float32,
                )
                got = (got * inv).astype(jnp.bfloat16)
                for k in range(step // DH):
                    pieces[part, at // DH + k] = got[:, k * DH:(k + 1) * DH]
                at += step
        for h in range(heads):
            q, k, v = pieces[0, h], pieces[1, h], pieces[2, h]
            scores = lax.dot_general(
                q, k, (((1,), (1,)), ((), ())), preferred_element_type=jnp.float32
            ) * DH ** (-0.5)
            scores = jnp.where(masked, -1e30, scores)
            expo = jnp.exp(scores - jnp.max(scores, axis=-1, keepdims=True))
            weights = (expo / jnp.sum(expo, axis=-1, keepdims=True)).astype(jnp.bfloat16)
            mixed = jnp.dot(weights, v, preferred_element_type=jnp.float32)
            out_ref[:, h * DH:(h + 1) * DH] = mixed.astype(jnp.bfloat16)


def attend(ids, lengths, live, inv, table, heads, vocab):
    sets, seq = ids.shape
    width = heads * DH
    grid_spec = pltpu.PrefetchScalarGridSpec(
        num_scalar_prefetch=2,
        grid=(sets,),
        in_specs=[
            pl.BlockSpec((None, seq, 1), lambda s, *_: (s, 0, 0)),
            pl.BlockSpec((None, seq, 1), lambda s, *_: (s, 0, 0)),
            pl.BlockSpec((vocab + seq, 3 * width), lambda s, *_: (0, 0)),
        ],
        out_specs=pl.BlockSpec((seq, width), lambda s, *_: (s, 0)),
    )
    return pl.pallas_call(
        functools.partial(attend_kernel, heads, vocab),
        out_shape=jax.ShapeDtypeStruct((sets * seq, width), jnp.bfloat16),
        grid_spec=grid_spec,
        compiler_params=pltpu.CompilerParams(vmem_limit_bytes=40 * 1024 * 1024),
        cost_estimate=pl.CostEstimate(
            flops=2 * sets * seq * (vocab + seq) * 3 * width,
            bytes_accessed=2 * (vocab + seq) * 3 * width,
            transcendentals=sets * seq * seq * heads,
        ),
    )(lengths, live, ids[..., None], inv[..., None], table)


def on_device(
    token_ids, set_lengths, live_counts, embed_table, position_table, norm_gain,
    w_query, w_key, w_value, w_out,
):
    sets, seq = token_ids.shape
    vocab, d = embed_table.shape
    me, part = lax.axis_index("row"), lax.axis_index("mp")
    depth, width = w_query.shape
    heads = width // DH

    rows = jnp.concatenate([
        lax.dynamic_slice_in_dim(embed_table, me * depth, depth, 1),
        lax.dynamic_slice_in_dim(position_table, me * depth, depth, 1),
    ], axis=0).astype(jnp.float32)
    rows = (rows * lax.dynamic_slice_in_dim(norm_gain, me * depth, depth)).astype(jnp.bfloat16)
    partial = jnp.concatenate([
        jnp.dot(rows, w, preferred_element_type=jnp.float32).astype(jnp.bfloat16)
        for w in (w_query, w_key, w_value)
    ], axis=1)
    table = lax.psum(partial, "row")

    out_full = lax.all_gather(w_out, "row", axis=1, tiled=True)

    pick = (token_ids.reshape(-1, 1) == jnp.arange(vocab)[None]).astype(jnp.bfloat16)
    picked = jnp.dot(pick, embed_table, preferred_element_type=jnp.float32)
    stored = (
        picked.reshape(sets, seq, d) + position_table.astype(jnp.float32)[None]
    ).astype(jnp.bfloat16)
    widened = stored.astype(jnp.float32)
    inv = lax.rsqrt(jnp.mean(widened * widened, axis=-1) + 1e-05)

    live = jnp.arange(sets) < live_counts[me]
    mixed = attend(
        token_ids, set_lengths, live.astype(jnp.int32), inv, table, heads, vocab
    )
    partial_out = jnp.dot(mixed, out_full, preferred_element_type=jnp.float32).astype(jnp.bfloat16)
    summed = lax.psum_scatter(
        partial_out, "mp", scatter_dimension=1, tiled=True
    ).astype(jnp.float32)
    features = summed.shape[1]
    residual = lax.dynamic_slice_in_dim(
        stored.reshape(sets * seq, d), part * features, features, 1
    ).astype(jnp.float32)
    valid = jnp.arange(seq)[None, :] < set_lengths[:, None]
    keep = (live[:, None] & valid).reshape(-1, 1)
    output = jnp.where(keep, residual + summed, 0.0).astype(jnp.bfloat16)
    return output.reshape(sets, seq, features)


def solution(mesh):
    in_specs = (
        P("row", None), P("row"), P(), P(), P(), P(),
        P("row", "mp"), P("row", "mp"), P("row", "mp"), P("mp", "row"),
    )
    return jax.shard_map(
        on_device, mesh=mesh, in_specs=in_specs, out_specs=P("row", None, "mp"), check_vma=False
    )
```

```python
import functools
import jax
import jax.numpy as jnp
from jax import lax
from jax.experimental import pallas as pl
from jax.experimental.pallas import tpu as pltpu
from jax.sharding import PartitionSpec as P

DH = 128


def attend_kernel(heads, vocab, lengths_ref, live_ref, ids_ref, inv_ref, table_ref, out_ref):
    s = pl.program_id(0)
    seq = out_ref.shape[0]
    width = heads * DH
    length = lengths_ref[s]

    @pl.when(live_ref[s] == 0)
    def _():
        out_ref[...] = jnp.zeros_like(out_ref)

    @pl.when(live_ref[s] != 0)
    def _():
        ids = ids_ref[...].reshape(seq, 1)
        cols = lax.broadcasted_iota(jnp.int32, (seq, vocab + seq), 1)
        rows = lax.broadcasted_iota(jnp.int32, (seq, vocab + seq), 0)
        pick = jnp.where((cols == ids) | (cols == rows + vocab), 1.0, 0.0).astype(jnp.bfloat16)
        inv = inv_ref[...].reshape(seq, 1)
        masked = lax.broadcasted_iota(jnp.int32, (seq, seq), 1) >= length


        pieces = {}
        for part in range(3):
            at = 0
            while at < width:
                step = min(2 * DH, width - at)
                got = jnp.dot(
                    pick, table_ref[:vocab + seq, part * width + at:part * width + at + step],
                    preferred_element_type=jnp.float32,
                )
                got = (got * inv).astype(jnp.bfloat16)
                for k in range(step // DH):
                    pieces[part, at // DH + k] = got[:, k * DH:(k + 1) * DH]
                at += step
        for h in range(heads):
            q, k, v = pieces[0, h], pieces[1, h], pieces[2, h]
            scores = lax.dot_general(
                q, k, (((1,), (1,)), ((), ())), preferred_element_type=jnp.float32
            ) * DH ** (-0.5)
            scores = jnp.where(masked, -1e30, scores)
            expo = jnp.exp(scores - jnp.max(scores, axis=-1, keepdims=True))
            weights = (expo / jnp.sum(expo, axis=-1, keepdims=True)).astype(jnp.bfloat16)
            mixed = jnp.dot(weights, v, preferred_element_type=jnp.float32)
            out_ref[:, h * DH:(h + 1) * DH] = mixed.astype(jnp.bfloat16)


def attend(ids, lengths, live, inv, table, heads, vocab):
    sets, seq = ids.shape
    width = heads * DH
    grid_spec = pltpu.PrefetchScalarGridSpec(
        num_scalar_prefetch=2,
        grid=(sets,),
        in_specs=[
            pl.BlockSpec((None, seq, 1), lambda s, *_: (s, 0, 0)),
            pl.BlockSpec((None, seq, 1), lambda s, *_: (s, 0, 0)),
            pl.BlockSpec(table.shape, lambda s, *_: (0, 0)),
        ],
        out_specs=pl.BlockSpec((seq, width), lambda s, *_: (s, 0)),
    )
    return pl.pallas_call(
        functools.partial(attend_kernel, heads, vocab),
        out_shape=jax.ShapeDtypeStruct((sets * seq, width), jnp.bfloat16),
        grid_spec=grid_spec,
        compiler_params=pltpu.CompilerParams(vmem_limit_bytes=40 * 1024 * 1024),
        cost_estimate=pl.CostEstimate(
            flops=2 * sets * seq * (vocab + seq) * 3 * width,
            bytes_accessed=2 * (vocab + seq) * 3 * width,
            transcendentals=sets * seq * seq * heads,
        ),
    )(lengths, live, ids[..., None], inv[..., None], table)


def flip(me, bit):
    return me + (1 - 2 * (lax.rem(me // (1 << bit), 2))) * (1 << bit)


def sum_kernel(levels, chunk, part_ref, out_ref, land, acc, send_sem, recv_sem):
    me = lax.axis_index("row")
    rows, cols = part_ref.shape
    chunks = cols // chunk
    count = len(levels)

    barrier = pltpu.get_barrier_semaphore()
    for bit in range(count):
        pl.semaphore_signal(
            barrier, inc=1, device_id={"row": flip(me, bit)}, device_id_type=pl.DeviceIdType.MESH
        )
    pl.semaphore_wait(barrier, count)

    def order(c):
        return levels if c % 2 == 0 else (levels[1], levels[0]) + levels[2:]

    def span(c, level):
        low, size = 0, rows
        for bit in order(c)[:level]:
            size = size // 2
            low = low + lax.rem(me // (1 << bit), 2) * size
        return low, size

    def remote(c, stage, src, dst, bit):
        return pltpu.make_async_remote_copy(
            src_ref=src, dst_ref=dst,
            send_sem=send_sem.at[c, stage], recv_sem=recv_sem.at[c, stage],
            device_id={"row": flip(me, bit)}, device_id_type=pl.DeviceIdType.MESH,
        )

    flying = {}

    def start(c, stage):
        at = pl.ds(c * chunk, chunk)
        if stage < count:
            level, bit = stage, order(c)[stage]
            low, size = span(c, level)
            half = size // 2
            theirs = low + (1 - lax.rem(me // (1 << bit), 2)) * half
            src = (part_ref if level == 0 else acc).at[pl.ds(pl.multiple_of(theirs, 16), half), at]
            dst = land.at[pl.ds(rows - size, half), at]
        else:
            level = 2 * count - 1 - stage
            bit = order(c)[level]
            low, size = span(c, level + 1)
            src = out_ref.at[pl.ds(pl.multiple_of(low, 16), size), at]
            dst = src
        flying[c, stage] = remote(c, stage, src, dst, bit)
        flying[c, stage].start()

    def finish(c, stage):
        flying[c, stage].wait()
        if stage < count:
            at = pl.ds(c * chunk, chunk)
            low, size = span(c, stage + 1)
            here = pl.ds(pl.multiple_of(low, 16), size)
            mine = (part_ref if stage == 0 else acc)[here, at].astype(jnp.float32)
            got = land[pl.ds(rows - 2 * size, size), at].astype(jnp.float32)
            total = (mine + got).astype(jnp.bfloat16)
            if stage == count - 1:
                out_ref[here, at] = total
            else:
                acc[here, at] = total

    ahead = 4
    for c in range(min(ahead, chunks)):
        start(c, 0)
    for step in range(2 * count + (chunks - 1) // 2):
        for c in range(chunks):
            stage = step - c // 2
            if 0 <= stage < 2 * count:
                finish(c, stage)
                if stage + 1 < 2 * count:
                    start(c, stage + 1)
                if stage == 0 and c + ahead < chunks:
                    start(c + ahead, 0)


def sum_over_rows(partial, row_count):
    rows, cols = partial.shape
    levels = tuple(range(row_count.bit_length() - 1))
    count = len(levels)
    chunk = 640 if cols % 640 == 0 else 128
    chunks = cols // chunk
    whole = pl.BlockSpec(memory_space=pltpu.VMEM)
    return pl.pallas_call(
        functools.partial(sum_kernel, levels, chunk),
        out_shape=jax.ShapeDtypeStruct((rows, cols), jnp.bfloat16),
        in_specs=[whole],
        out_specs=whole,
        scratch_shapes=[
            pltpu.VMEM((rows, cols), jnp.bfloat16),
            pltpu.VMEM((rows, cols), jnp.bfloat16),
            pltpu.SemaphoreType.DMA((chunks, 2 * count)),
            pltpu.SemaphoreType.DMA((chunks, 2 * count)),
        ],
        compiler_params=pltpu.CompilerParams(
            collective_id=0, has_side_effects=True, vmem_limit_bytes=40 * 1024 * 1024
        ),
        cost_estimate=pl.CostEstimate(
            flops=2 * rows * cols, bytes_accessed=200 * rows * cols, transcendentals=0
        ),
    )(partial)


def on_device(
    row_count, token_ids, set_lengths, live_counts, embed_table, position_table, norm_gain,
    w_query, w_key, w_value, w_out,
):
    sets, seq = token_ids.shape
    vocab, d = embed_table.shape
    me, part = lax.axis_index("row"), lax.axis_index("mp")
    depth, width = w_query.shape
    heads = width // DH

    rows = jnp.concatenate([
        lax.dynamic_slice_in_dim(embed_table, me * depth, depth, 1),
        lax.dynamic_slice_in_dim(position_table, me * depth, depth, 1),
    ], axis=0).astype(jnp.float32)
    rows = (rows * lax.dynamic_slice_in_dim(norm_gain, me * depth, depth)).astype(jnp.bfloat16)
    short = -rows.shape[0] % (16 * row_count)
    if short:
        rows = jnp.pad(rows, ((0, short), (0, 0)))
    partial = jnp.concatenate([
        jnp.dot(rows, w, preferred_element_type=jnp.float32).astype(jnp.bfloat16)
        for w in (w_query, w_key, w_value)
    ], axis=1)
    table = sum_over_rows(partial, row_count)

    out_full = lax.all_gather(w_out, "row", axis=1, tiled=True)

    pick = (token_ids.reshape(-1, 1) == jnp.arange(vocab)[None]).astype(jnp.bfloat16)
    picked = jnp.dot(pick, embed_table, preferred_element_type=jnp.float32)
    stored = (
        picked.reshape(sets, seq, d) + position_table.astype(jnp.float32)[None]
    ).astype(jnp.bfloat16)
    widened = stored.astype(jnp.float32)
    inv = lax.rsqrt(jnp.mean(widened * widened, axis=-1) + 1e-05)

    live = jnp.arange(sets) < live_counts[me]
    mixed = attend(
        token_ids, set_lengths, live.astype(jnp.int32), inv, table, heads, vocab
    )
    partial_out = jnp.dot(mixed, out_full, preferred_element_type=jnp.float32).astype(jnp.bfloat16)
    summed = lax.psum_scatter(
        partial_out, "mp", scatter_dimension=1, tiled=True
    ).astype(jnp.float32)
    features = summed.shape[1]
    residual = lax.dynamic_slice_in_dim(
        stored.reshape(sets * seq, d), part * features, features, 1
    ).astype(jnp.float32)
    valid = jnp.arange(seq)[None, :] < set_lengths[:, None]
    keep = (live[:, None] & valid).reshape(-1, 1)
    output = jnp.where(keep, residual + summed, 0.0).astype(jnp.bfloat16)
    return output.reshape(sets, seq, features)


def solution(mesh):
    in_specs = (
        P("row", None), P("row"), P(), P(), P(), P(),
        P("row", "mp"), P("row", "mp"), P("row", "mp"), P("mp", "row"),
    )
    return jax.shard_map(
        functools.partial(on_device, mesh.shape["row"]), mesh=mesh, in_specs=in_specs, out_specs=P("row", None, "mp"), check_vma=False
    )
```

```python
import functools
import jax
import jax.numpy as jnp
from jax import lax
from jax.experimental import pallas as pl
from jax.experimental.pallas import tpu as pltpu
from jax.sharding import PartitionSpec as P

DH = 128


def attend_kernel(heads, vocab, lengths_ref, live_ref, ids_ref, inv_ref, table_ref, out_ref):
    s = pl.program_id(0)
    seq = out_ref.shape[0]
    width = heads * DH
    length = lengths_ref[s]

    @pl.when(live_ref[s] == 0)
    def _():
        out_ref[...] = jnp.zeros_like(out_ref)

    @pl.when(live_ref[s] != 0)
    def _():
        ids = ids_ref[...].reshape(seq, 1)
        cols = lax.broadcasted_iota(jnp.int32, (seq, vocab + seq), 1)
        rows = lax.broadcasted_iota(jnp.int32, (seq, vocab + seq), 0)
        pick = jnp.where((cols == ids) | (cols == rows + vocab), 1.0, 0.0).astype(jnp.bfloat16)
        inv = inv_ref[...].reshape(seq, 1)
        masked = lax.broadcasted_iota(jnp.int32, (seq, seq), 1) >= length


        pieces = {}
        for part in range(3):
            at = 0
            while at < width:
                step = min(2 * DH, width - at)
                got = jnp.dot(
                    pick, table_ref[:vocab + seq, part * width + at:part * width + at + step],
                    preferred_element_type=jnp.float32,
                )
                got = (got * inv).astype(jnp.bfloat16)
                for k in range(step // DH):
                    pieces[part, at // DH + k] = got[:, k * DH:(k + 1) * DH]
                at += step
        for h in range(heads):
            q, k, v = pieces[0, h], pieces[1, h], pieces[2, h]
            scores = lax.dot_general(
                q, k, (((1,), (1,)), ((), ())), preferred_element_type=jnp.float32
            ) * DH ** (-0.5)
            scores = jnp.where(masked, -1e30, scores)
            expo = jnp.exp(scores - jnp.max(scores, axis=-1, keepdims=True))
            weights = (expo / jnp.sum(expo, axis=-1, keepdims=True)).astype(jnp.bfloat16)
            mixed = jnp.dot(weights, v, preferred_element_type=jnp.float32)
            out_ref[:, h * DH:(h + 1) * DH] = mixed.astype(jnp.bfloat16)


def attend(ids, lengths, live, inv, table, heads, vocab):
    sets, seq = ids.shape
    width = heads * DH
    grid_spec = pltpu.PrefetchScalarGridSpec(
        num_scalar_prefetch=2,
        grid=(sets,),
        in_specs=[
            pl.BlockSpec((None, seq, 1), lambda s, *_: (s, 0, 0)),
            pl.BlockSpec((None, seq, 1), lambda s, *_: (s, 0, 0)),
            pl.BlockSpec(table.shape, lambda s, *_: (0, 0)),
        ],
        out_specs=pl.BlockSpec((seq, width), lambda s, *_: (s, 0)),
    )
    return pl.pallas_call(
        functools.partial(attend_kernel, heads, vocab),
        out_shape=jax.ShapeDtypeStruct((sets * seq, width), jnp.bfloat16),
        grid_spec=grid_spec,
        compiler_params=pltpu.CompilerParams(vmem_limit_bytes=40 * 1024 * 1024),
        cost_estimate=pl.CostEstimate(
            flops=2 * sets * seq * (vocab + seq) * 3 * width,
            bytes_accessed=2 * (vocab + seq) * 3 * width,
            transcendentals=sets * seq * seq * heads,
        ),
    )(lengths, live, ids[..., None], inv[..., None], table)


def flip(me, bit):
    return me + (1 - 2 * (lax.rem(me // (1 << bit), 2))) * (1 << bit)


def sum_kernel(levels, chunk, part_ref, out_ref, land, acc, send_sem, recv_sem):
    me = lax.axis_index("row")
    rows, cols = part_ref.shape
    chunks = cols // chunk
    count = len(levels)

    barrier = pltpu.get_barrier_semaphore()
    for bit in range(count):
        pl.semaphore_signal(
            barrier, inc=1, device_id={"row": flip(me, bit)}, device_id_type=pl.DeviceIdType.MESH
        )
    pl.semaphore_wait(barrier, count)

    def order(c):
        return levels if c % 2 == 0 else (levels[1], levels[0]) + levels[2:]

    def span(c, level):
        low, size = 0, rows
        for bit in order(c)[:level]:
            size = size // 2
            low = low + lax.rem(me // (1 << bit), 2) * size
        return low, size

    def remote(c, stage, src, dst, bit):
        return pltpu.make_async_remote_copy(
            src_ref=src, dst_ref=dst,
            send_sem=send_sem.at[c, stage], recv_sem=recv_sem.at[c, stage],
            device_id={"row": flip(me, bit)}, device_id_type=pl.DeviceIdType.MESH,
        )

    flying = {}

    def start(c, stage):
        at = pl.ds(c * chunk, chunk)
        if stage < count:
            level, bit = stage, order(c)[stage]
            low, size = span(c, level)
            half = size // 2
            theirs = low + (1 - lax.rem(me // (1 << bit), 2)) * half
            src = (part_ref if level == 0 else acc).at[pl.ds(pl.multiple_of(theirs, 16), half), at]
            dst = land.at[pl.ds(rows - size, half), at]
        else:
            level = 2 * count - 1 - stage
            bit = order(c)[level]
            low, size = span(c, level + 1)
            src = out_ref.at[pl.ds(pl.multiple_of(low, 16), size), at]
            dst = src
        flying[c, stage] = remote(c, stage, src, dst, bit)
        flying[c, stage].start()

    def finish(c, stage):
        flying[c, stage].wait()
        if stage < count:
            at = pl.ds(c * chunk, chunk)
            low, size = span(c, stage + 1)
            here = pl.ds(pl.multiple_of(low, 16), size)
            mine = (part_ref if stage == 0 else acc)[here, at].astype(jnp.float32)
            got = land[pl.ds(rows - 2 * size, size), at].astype(jnp.float32)
            total = (mine + got).astype(jnp.bfloat16)
            if stage == count - 1:
                out_ref[here, at] = total
            else:
                acc[here, at] = total

    ahead = 4
    for c in range(min(ahead, chunks)):
        start(c, 0)
    for step in range(2 * count + (chunks - 1) // 2):
        for c in range(chunks):
            stage = step - c // 2
            if 0 <= stage < 2 * count:
                finish(c, stage)
                if stage + 1 < 2 * count:
                    start(c, stage + 1)
                if stage == 0 and c + ahead < chunks:
                    start(c + ahead, 0)


def sum_over_rows(partial, row_count):
    rows, cols = partial.shape
    levels = tuple(range(row_count.bit_length() - 1))
    count = len(levels)
    chunk = 640 if cols % 640 == 0 else 128
    chunks = cols // chunk
    whole = pl.BlockSpec(memory_space=pltpu.VMEM)
    return pl.pallas_call(
        functools.partial(sum_kernel, levels, chunk),
        out_shape=jax.ShapeDtypeStruct((rows, cols), jnp.bfloat16),
        in_specs=[whole],
        out_specs=whole,
        scratch_shapes=[
            pltpu.VMEM((rows, cols), jnp.bfloat16),
            pltpu.VMEM((rows, cols), jnp.bfloat16),
            pltpu.SemaphoreType.DMA((chunks, 2 * count)),
            pltpu.SemaphoreType.DMA((chunks, 2 * count)),
        ],
        compiler_params=pltpu.CompilerParams(
            collective_id=0, has_side_effects=True, vmem_limit_bytes=40 * 1024 * 1024
        ),
        cost_estimate=pl.CostEstimate(
            flops=2 * rows * cols, bytes_accessed=200 * rows * cols, transcendentals=0
        ),
    )(partial)


def bit_of(index, bit):
    return lax.rem(index // (1 << bit), 2)


class Scatter:
    def __init__(self, part, count, mixed, weight, out, buf, land, send_sem, recv_sem):
        self.part, self.count = part, count
        self.mixed, self.weight, self.out = mixed, weight, out
        self.buf, self.land = buf, land
        self.send_sem, self.recv_sem = send_sem, recv_sem
        self.chunks, self.half, self.rows, self.width = buf.shape
        self.flying = {}

    def product(self, c, mine, finish):
        features = self.chunks * self.width
        tile = min(256, self.rows)
        first = bit_of(self.part, 0)
        first = first if mine else 1 - first
        for p in range(self.half):
            block = first
            for i in range(1, self.count):
                block = block + (1 << i) * ((p >> (self.count - 1 - i)) & 1)
            at = pl.multiple_of(block * features + c * self.width, 128)

            @pl.loop(0, self.rows // tile)
            def _(t):
                here = pl.ds(pl.multiple_of(t * tile, tile), tile)
                got = jnp.dot(
                    self.mixed[here, :], self.weight[:, pl.ds(at, self.width)],
                    preferred_element_type=jnp.float32,
                )
                if mine:
                    got = got + self.land[c, p, here, :].astype(jnp.float32)
                finish(c, p, here, got.astype(jnp.bfloat16))

    def kept(self, level):
        low, size = 0, self.half
        for bit in range(1, level + 1):
            size = size // 2
            low = low + bit_of(self.part, bit) * size
        return low, size

    def start(self, c, level):
        if level == 0:
            def store(c, p, here, value):
                self.buf[c, p, here, :] = value
            self.product(c, False, store)
            src, dst = self.buf.at[c], self.land.at[c, pl.ds(0, self.half)]
        else:
            low, size = self.kept(level - 1)
            size = size // 2
            theirs = low + (1 - bit_of(self.part, level)) * size
            src = self.buf.at[c, pl.ds(theirs, size)]
            dst = self.land.at[c, pl.ds(2 * self.half - 2 * size, size)]
        copy = pltpu.make_async_remote_copy(
            src_ref=src, dst_ref=dst,
            send_sem=self.send_sem.at[c, level], recv_sem=self.recv_sem.at[c, level],
            device_id={"mp": flip(self.part, level)}, device_id_type=pl.DeviceIdType.MESH,
        )
        copy.start()
        self.flying[c, level] = copy

    def finish(self, c, level):
        self.flying[c, level].wait()
        last = level == self.count - 1
        columns = pl.ds(c * self.width, self.width)
        if level == 0:
            def store(c, p, here, value):
                if last:
                    self.out[here, columns] = value
                else:
                    self.buf[c, p, here, :] = value
            self.product(c, True, store)
        else:
            low, size = self.kept(level)
            tile = min(256, self.rows)
            for k in range(size):
                @pl.loop(0, self.rows // tile)
                def _(t):
                    here = pl.ds(pl.multiple_of(t * tile, tile), tile)
                    got = self.land[c, 2 * self.half - 2 * size + k, here, :].astype(jnp.float32)
                    value = (self.buf[c, low + k, here, :].astype(jnp.float32) + got).astype(jnp.bfloat16)
                    if last:
                        self.out[here, columns] = value
                    else:
                        self.buf[c, low + k, here, :] = value

    def advance(self, step):
        if step < self.chunks:
            self.start(step, 0)
        for level in range(self.count):
            c = step - 1 - level
            if 0 <= c < self.chunks:
                self.finish(c, level)
                if level + 1 < self.count:
                    self.start(c, level + 1)

    def steps(self):
        return self.chunks + self.count


def scatter_kernel(count, mixed_ref, weight_ref, out_ref, buf, land, send_sem, recv_sem):
    part = lax.axis_index("mp")
    barrier = pltpu.get_barrier_semaphore()
    for bit in range(count):
        pl.semaphore_signal(
            barrier, inc=1, device_id={"mp": flip(part, bit)}, device_id_type=pl.DeviceIdType.MESH
        )
    pl.semaphore_wait(barrier, count)
    work = Scatter(part, count, mixed_ref, weight_ref, out_ref, buf, land, send_sem, recv_sem)
    for step in range(work.steps()):
        work.advance(step)


def project_out(mixed, weight, part_count):
    rows = mixed.shape[0]
    features = weight.shape[1] // part_count
    count = part_count.bit_length() - 1
    chunks = 5 if features % 640 == 0 else 1
    width = features // chunks
    half = part_count // 2
    whole = pl.BlockSpec(memory_space=pltpu.VMEM)
    return pl.pallas_call(
        functools.partial(scatter_kernel, count),
        out_shape=jax.ShapeDtypeStruct((rows, features), jnp.bfloat16),
        in_specs=[whole, whole],
        out_specs=whole,
        scratch_shapes=[
            pltpu.VMEM((chunks, half, rows, width), jnp.bfloat16),
            pltpu.VMEM((chunks, 2 * half - 1, rows, width), jnp.bfloat16),
            pltpu.SemaphoreType.DMA((chunks, count)),
            pltpu.SemaphoreType.DMA((chunks, count)),
        ],
        compiler_params=pltpu.CompilerParams(
            collective_id=1, has_side_effects=True, vmem_limit_bytes=56 * 1024 * 1024
        ),
        cost_estimate=pl.CostEstimate(
            flops=2 * rows * mixed.shape[1] * weight.shape[1],
            bytes_accessed=2 * weight.size, transcendentals=0,
        ),
    )(mixed, weight)


def on_device(
    row_count, part_count, token_ids, set_lengths, live_counts, embed_table, position_table, norm_gain,
    w_query, w_key, w_value, w_out,
):
    sets, seq = token_ids.shape
    vocab, d = embed_table.shape
    me, part = lax.axis_index("row"), lax.axis_index("mp")
    depth, width = w_query.shape
    heads = width // DH

    rows = jnp.concatenate([
        lax.dynamic_slice_in_dim(embed_table, me * depth, depth, 1),
        lax.dynamic_slice_in_dim(position_table, me * depth, depth, 1),
    ], axis=0).astype(jnp.float32)
    rows = (rows * lax.dynamic_slice_in_dim(norm_gain, me * depth, depth)).astype(jnp.bfloat16)
    short = -rows.shape[0] % (16 * row_count)
    if short:
        rows = jnp.pad(rows, ((0, short), (0, 0)))
    partial = jnp.concatenate([
        jnp.dot(rows, w, preferred_element_type=jnp.float32).astype(jnp.bfloat16)
        for w in (w_query, w_key, w_value)
    ], axis=1)
    table = sum_over_rows(partial, row_count)

    out_full = lax.all_gather(w_out, "row", axis=1, tiled=True)

    pick = (token_ids.reshape(-1, 1) == jnp.arange(vocab)[None]).astype(jnp.bfloat16)
    picked = jnp.dot(pick, embed_table, preferred_element_type=jnp.float32)
    stored = (
        picked.reshape(sets, seq, d) + position_table.astype(jnp.float32)[None]
    ).astype(jnp.bfloat16)
    widened = stored.astype(jnp.float32)
    inv = lax.rsqrt(jnp.mean(widened * widened, axis=-1) + 1e-05)

    live = jnp.arange(sets) < live_counts[me]
    mixed = attend(
        token_ids, set_lengths, live.astype(jnp.int32), inv, table, heads, vocab
    )
    summed = project_out(mixed, out_full, part_count).astype(jnp.float32)
    features = summed.shape[1]
    residual = lax.dynamic_slice_in_dim(
        stored.reshape(sets * seq, d), part * features, features, 1
    ).astype(jnp.float32)
    valid = jnp.arange(seq)[None, :] < set_lengths[:, None]
    keep = (live[:, None] & valid).reshape(-1, 1)
    output = jnp.where(keep, residual + summed, 0.0).astype(jnp.bfloat16)
    return output.reshape(sets, seq, features)


def solution(mesh):
    in_specs = (
        P("row", None), P("row"), P(), P(), P(), P(),
        P("row", "mp"), P("row", "mp"), P("row", "mp"), P("mp", "row"),
    )
    return jax.shard_map(
        functools.partial(on_device, mesh.shape["row"], mesh.shape["mp"]), mesh=mesh, in_specs=in_specs, out_specs=P("row", None, "mp"), check_vma=False
    )
```

```python
import functools
import jax
import jax.numpy as jnp
from jax import lax
from jax.experimental import pallas as pl
from jax.experimental.pallas import tpu as pltpu
from jax.sharding import PartitionSpec as P

DH = 128


def attend_set(heads, vocab, ids, inv, masked, table_ref, store):
    seq = ids.shape[0]
    width = heads * DH
    cols = lax.broadcasted_iota(jnp.int32, (seq, vocab + seq), 1)
    rows = lax.broadcasted_iota(jnp.int32, (seq, vocab + seq), 0)
    pick = jnp.where((cols == ids) | (cols == rows + vocab), 1.0, 0.0).astype(jnp.bfloat16)
    pieces = {}
    for part in range(3):
        at = 0
        while at < width:
            step = min(2 * DH, width - at)
            got = jnp.dot(
                pick, table_ref[:vocab + seq, part * width + at:part * width + at + step],
                preferred_element_type=jnp.float32,
            )
            got = (got * inv).astype(jnp.bfloat16)
            for k in range(step // DH):
                pieces[part, at // DH + k] = got[:, k * DH:(k + 1) * DH]
            at += step
    for h in range(heads):
        q, k, v = pieces[0, h], pieces[1, h], pieces[2, h]
        scores = lax.dot_general(
            q, k, (((1,), (1,)), ((), ())), preferred_element_type=jnp.float32
        ) * DH ** (-0.5)
        scores = jnp.where(masked, -1e30, scores)
        expo = jnp.exp(scores - jnp.max(scores, axis=-1, keepdims=True))
        weights = (expo / jnp.sum(expo, axis=-1, keepdims=True)).astype(jnp.bfloat16)
        mixed = jnp.dot(weights, v, preferred_element_type=jnp.float32)
        store(h, mixed.astype(jnp.bfloat16))


def attend_kernel(heads, vocab, lengths_ref, live_ref, ids_ref, inv_ref, table_ref, out_ref):
    s = pl.program_id(0)
    seq = out_ref.shape[0]
    width = heads * DH
    length = lengths_ref[s]

    @pl.when(live_ref[s] == 0)
    def _():
        out_ref[...] = jnp.zeros_like(out_ref)

    @pl.when(live_ref[s] != 0)
    def _():
        masked = lax.broadcasted_iota(jnp.int32, (seq, seq), 1) >= length

        def store(h, value):
            out_ref[:, h * DH:(h + 1) * DH] = value

        attend_set(
            heads, vocab, ids_ref[...].reshape(seq, 1), inv_ref[...].reshape(seq, 1), masked,
            table_ref, store,
        )


def attend(ids, lengths, live, inv, table, heads, vocab):
    sets, seq = ids.shape
    width = heads * DH
    grid_spec = pltpu.PrefetchScalarGridSpec(
        num_scalar_prefetch=2,
        grid=(sets,),
        in_specs=[
            pl.BlockSpec((None, seq, 1), lambda s, *_: (s, 0, 0)),
            pl.BlockSpec((None, seq, 1), lambda s, *_: (s, 0, 0)),
            pl.BlockSpec(table.shape, lambda s, *_: (0, 0)),
        ],
        out_specs=pl.BlockSpec((seq, width), lambda s, *_: (s, 0)),
    )
    return pl.pallas_call(
        functools.partial(attend_kernel, heads, vocab),
        out_shape=jax.ShapeDtypeStruct((sets * seq, width), jnp.bfloat16),
        grid_spec=grid_spec,
        compiler_params=pltpu.CompilerParams(vmem_limit_bytes=40 * 1024 * 1024),
        cost_estimate=pl.CostEstimate(
            flops=2 * sets * seq * (vocab + seq) * 3 * width,
            bytes_accessed=2 * (vocab + seq) * 3 * width,
            transcendentals=sets * seq * seq * heads,
        ),
    )(lengths, live, ids[..., None], inv[..., None], table)


def bit_of(index, bit):
    return lax.rem(index // (1 << bit), 2)


def flip(me, bit):
    return me + (1 - 2 * (lax.rem(me // (1 << bit), 2))) * (1 << bit)


class RowSum:
    def __init__(self, me, levels, chunk, part, out, land, acc, send_sem, recv_sem):
        self.me, self.levels, self.chunk = me, levels, chunk
        self.part, self.out, self.land, self.acc = part, out, land, acc
        self.send_sem, self.recv_sem = send_sem, recv_sem
        self.rows, cols = part.shape
        self.chunks, self.count = cols // chunk, len(levels)
        self.flying = {}

    def order(self, c):
        levels = self.levels
        return levels if c % 2 == 0 else (levels[1], levels[0]) + levels[2:]

    def span(self, c, level):
        low, size = 0, self.rows
        for bit in self.order(c)[:level]:
            size = size // 2
            low = low + bit_of(self.me, bit) * size
        return low, size

    def start(self, c, stage):
        at = pl.ds(c * self.chunk, self.chunk)
        if stage < self.count:
            level, bit = stage, self.order(c)[stage]
            low, size = self.span(c, level)
            half = size // 2
            theirs = low + (1 - bit_of(self.me, bit)) * half
            held = self.part if level == 0 else self.acc
            src = held.at[pl.ds(pl.multiple_of(theirs, 16), half), at]
            dst = self.land.at[pl.ds(self.rows - size, half), at]
        else:
            level = 2 * self.count - 1 - stage
            bit = self.order(c)[level]
            low, size = self.span(c, level + 1)
            src = self.out.at[pl.ds(pl.multiple_of(low, 16), size), at]
            dst = src
        copy = pltpu.make_async_remote_copy(
            src_ref=src, dst_ref=dst,
            send_sem=self.send_sem.at[c, stage], recv_sem=self.recv_sem.at[c, stage],
            device_id={"row": flip(self.me, bit)}, device_id_type=pl.DeviceIdType.MESH,
        )
        copy.start()
        self.flying[c, stage] = copy

    def finish(self, c, stage):
        self.flying[c, stage].wait()
        if stage < self.count:
            at = pl.ds(c * self.chunk, self.chunk)
            low, size = self.span(c, stage + 1)
            here = pl.ds(pl.multiple_of(low, 16), size)
            mine = (self.part if stage == 0 else self.acc)[here, at].astype(jnp.float32)
            got = self.land[pl.ds(self.rows - 2 * size, size), at].astype(jnp.float32)
            total = (mine + got).astype(jnp.bfloat16)
            if stage == self.count - 1:
                self.out[here, at] = total
            else:
                self.acc[here, at] = total

    def run(self, beside=None):
        stages, ahead = 2 * self.count, 4
        for c in range(min(ahead, self.chunks)):
            self.start(c, 0)
        for step in range(stages + (self.chunks - 1) // 2):
            if beside is not None and step == self.count:
                beside()
            for c in range(self.chunks):
                stage = step - c // 2
                if 0 <= stage < stages:
                    self.finish(c, stage)
                    if stage + 1 < stages:
                        self.start(c, stage + 1)
                    if stage == 0 and c + ahead < self.chunks:
                        self.start(c + ahead, 0)


def greet(me, count, part, part_count):
    barrier = pltpu.get_barrier_semaphore()
    for bit in range(count):
        pl.semaphore_signal(
            barrier, inc=1, device_id={"row": flip(me, bit)}, device_id_type=pl.DeviceIdType.MESH
        )
    for bit in range(part_count):
        pl.semaphore_signal(
            barrier, inc=1, device_id={"mp": flip(part, bit)}, device_id_type=pl.DeviceIdType.MESH
        )
    pl.semaphore_wait(barrier, count + part_count)


def sum_kernel(levels, chunk, part_ref, out_ref, land, acc, send_sem, recv_sem):
    me = lax.axis_index("row")
    greet(me, len(levels), 0, 0)
    RowSum(me, levels, chunk, part_ref, out_ref, land, acc, send_sem, recv_sem).run()


def sum_over_rows(partial, row_count):
    rows, cols = partial.shape
    levels = tuple(range(row_count.bit_length() - 1))
    count = len(levels)
    chunk = 640 if cols % 640 == 0 else 128
    chunks = cols // chunk
    whole = pl.BlockSpec(memory_space=pltpu.VMEM)
    return pl.pallas_call(
        functools.partial(sum_kernel, levels, chunk),
        out_shape=jax.ShapeDtypeStruct((rows, cols), jnp.bfloat16),
        in_specs=[whole],
        out_specs=whole,
        scratch_shapes=[
            pltpu.VMEM((rows, cols), jnp.bfloat16),
            pltpu.VMEM((rows, cols), jnp.bfloat16),
            pltpu.SemaphoreType.DMA((chunks, 2 * count)),
            pltpu.SemaphoreType.DMA((chunks, 2 * count)),
        ],
        compiler_params=pltpu.CompilerParams(
            collective_id=0, has_side_effects=True, vmem_limit_bytes=40 * 1024 * 1024
        ),
        cost_estimate=pl.CostEstimate(
            flops=2 * rows * cols, bytes_accessed=200 * rows * cols, transcendentals=0
        ),
    )(partial)


class Scatter:
    def __init__(self, part, count, mixed, weight, out, buf, land, send_sem, recv_sem):
        self.part, self.count = part, count
        self.mixed, self.weight, self.out = mixed, weight, out
        self.buf, self.land = buf, land
        self.send_sem, self.recv_sem = send_sem, recv_sem
        self.chunks, self.half, self.rows, self.width = buf.shape
        self.flying = {}

    def columns(self, c, block):
        at = pl.multiple_of(block * self.chunks * self.width + c * self.width, 128)
        return self.weight[:, pl.ds(at, self.width)]

    def store(self, c, here, value):
        self.out[here, pl.ds(c * self.width, self.width)] = value

    def product(self, c, mine, finish):
        tile = min(256, self.rows)
        first = bit_of(self.part, 0)
        first = first if mine else 1 - first
        for p in range(self.half):
            block = first
            for i in range(1, self.count):
                block = block + (1 << i) * ((p >> (self.count - 1 - i)) & 1)
            load = functools.partial(self.columns, c, block)

            @pl.loop(0, self.rows // tile)
            def _(t):
                here = pl.ds(pl.multiple_of(t * tile, tile), tile)
                got = jnp.dot(
                    self.mixed[here, :], load(),
                    preferred_element_type=jnp.float32,
                )
                if mine:
                    got = got + self.land[c, p, here, :].astype(jnp.float32)
                finish(c, p, here, got.astype(jnp.bfloat16))

    def kept(self, level):
        low, size = 0, self.half
        for bit in range(1, level + 1):
            size = size // 2
            low = low + bit_of(self.part, bit) * size
        return low, size

    def start(self, c, level):
        if level == 0:
            def store(c, p, here, value):
                self.buf[c, p, here, :] = value
            self.product(c, False, store)
            src, dst = self.buf.at[c], self.land.at[c, pl.ds(0, self.half)]
        else:
            low, size = self.kept(level - 1)
            size = size // 2
            theirs = low + (1 - bit_of(self.part, level)) * size
            src = self.buf.at[c, pl.ds(theirs, size)]
            dst = self.land.at[c, pl.ds(2 * self.half - 2 * size, size)]
        copy = pltpu.make_async_remote_copy(
            src_ref=src, dst_ref=dst,
            send_sem=self.send_sem.at[c, level], recv_sem=self.recv_sem.at[c, level],
            device_id={"mp": flip(self.part, level)}, device_id_type=pl.DeviceIdType.MESH,
        )
        copy.start()
        self.flying[c, level] = copy

    def finish(self, c, level):
        self.flying[c, level].wait()
        last = level == self.count - 1
        if level == 0:
            def store(c, p, here, value):
                if last:
                    self.store(c, here, value)
                else:
                    self.buf[c, p, here, :] = value
            self.product(c, True, store)
        else:
            low, size = self.kept(level)
            tile = min(256, self.rows)
            for k in range(size):
                @pl.loop(0, self.rows // tile)
                def _(t):
                    here = pl.ds(pl.multiple_of(t * tile, tile), tile)
                    got = self.land[c, 2 * self.half - 2 * size + k, here, :].astype(jnp.float32)
                    value = (self.buf[c, low + k, here, :].astype(jnp.float32) + got).astype(jnp.bfloat16)
                    if last:
                        self.store(c, here, value)
                    else:
                        self.buf[c, low + k, here, :] = value

    def advance(self, step):
        if step < self.chunks:
            self.start(step, 0)
        for level in range(self.count):
            c = step - 1 - level
            if 0 <= c < self.chunks:
                self.finish(c, level)
                if level + 1 < self.count:
                    self.start(c, level + 1)

    def steps(self):
        return self.chunks + self.count


def scatter_kernel(count, mixed_ref, weight_ref, out_ref, buf, land, send_sem, recv_sem):
    part = lax.axis_index("mp")
    barrier = pltpu.get_barrier_semaphore()
    for bit in range(count):
        pl.semaphore_signal(
            barrier, inc=1, device_id={"mp": flip(part, bit)}, device_id_type=pl.DeviceIdType.MESH
        )
    pl.semaphore_wait(barrier, count)
    work = Scatter(part, count, mixed_ref, weight_ref, out_ref, buf, land, send_sem, recv_sem)
    for step in range(work.steps()):
        work.advance(step)


def project_out(mixed, weight, part_count):
    rows = mixed.shape[0]
    features = weight.shape[1] // part_count
    count = part_count.bit_length() - 1
    chunks = 5 if features % 640 == 0 else 1
    width = features // chunks
    half = part_count // 2
    whole = pl.BlockSpec(memory_space=pltpu.VMEM)
    return pl.pallas_call(
        functools.partial(scatter_kernel, count),
        out_shape=jax.ShapeDtypeStruct((rows, features), jnp.bfloat16),
        in_specs=[whole, whole],
        out_specs=whole,
        scratch_shapes=[
            pltpu.VMEM((chunks, half, rows, width), jnp.bfloat16),
            pltpu.VMEM((chunks, 2 * half - 1, rows, width), jnp.bfloat16),
            pltpu.SemaphoreType.DMA((chunks, count)),
            pltpu.SemaphoreType.DMA((chunks, count)),
        ],
        compiler_params=pltpu.CompilerParams(
            collective_id=1, has_side_effects=True, vmem_limit_bytes=56 * 1024 * 1024
        ),
        cost_estimate=pl.CostEstimate(
            flops=2 * rows * mixed.shape[1] * weight.shape[1],
            bytes_accessed=2 * weight.size, transcendentals=0,
        ),
    )(mixed, weight)


class Gather:
    def __init__(self, me, levels, held, send_sem, recv_sem):
        self.me, self.levels, self.held = me, levels, held
        self.send_sem, self.recv_sem = send_sem, recv_sem
        self.flying = {}

    def order(self, c):
        order = tuple(reversed(self.levels))
        return order if c % 2 == 0 else order[:-2] + (order[-1], order[-2])

    def start(self, c, level):
        order = self.order(c)
        to = flip(self.me, order[level])
        for i in range(1 << level):
            block = self.me
            for k in range(level):
                if (i >> k) & 1:
                    block = flip(block, order[k])
            slot = (1 << level) - 1 + i
            copy = pltpu.make_async_remote_copy(
                src_ref=self.held.at[c, block], dst_ref=self.held.at[c, block],
                send_sem=self.send_sem.at[c, slot], recv_sem=self.recv_sem.at[c, slot],
                device_id={"row": to}, device_id_type=pl.DeviceIdType.MESH,
            )
            copy.start()
            self.flying[c, slot] = copy

    def finish(self, c, level):
        for i in range(1 << level):
            self.flying[c, (1 << level) - 1 + i].wait()


class BlockScatter(Scatter):
    def columns(self, c, block):
        per = self.width // self.weight.shape[-1]
        return jnp.concatenate([self.weight[c, block * per + q] for q in range(per)], axis=1)

    def store(self, c, here, value):
        piece = self.weight.shape[-1]
        for q in range(self.width // piece):
            at = q * self.chunks * piece + c * piece
            self.out[here, pl.ds(at, piece)] = value[:, q * piece:(q + 1) * piece]


def whole_kernel(
    levels, count, heads, vocab, chunk, part_ref, w_ref, ids_ref, inv_ref, valid_ref, out_ref,
    table, land, acc, held, mixed, buf, land_out, row_sems, held_sems, out_sems,
):
    me, part = lax.axis_index("row"), lax.axis_index("mp")
    sets, seq, _ = ids_ref.shape
    chunks, _, _, piece = held.shape
    greet(me, len(levels), part, count)
    for c in range(chunks):
        held[c, me] = w_ref[:, c * piece:(c + 1) * piece]
    gather = Gather(me, levels, held, held_sems.at[0], held_sems.at[1])
    total = RowSum(me, levels, chunk, part_ref, table, land, acc, row_sems.at[0], row_sems.at[1])
    scatter = BlockScatter(part, count, mixed, held, out_ref, buf, land_out, out_sems.at[0], out_sems.at[1])
    last = len(levels) - 1

    def first():
        for c in range(chunks):
            gather.start(c, 0)

    total.run(first)
    for level in range(last - 1):
        for c in range(chunks):
            gather.finish(c, level)
            gather.start(c, level + 1)
    pairs = [tuple(range(c, min(c + 2, chunks))) for c in range(0, chunks, 2)]

    def move(pair, level):
        for c in pair:
            gather.finish(c, level)
            gather.start(c, level + 1)

    move(pairs[0], last - 1)

    @pl.loop(0, sets)
    def _(s):
        masked = jnp.broadcast_to(valid_ref[s], (seq, seq)) == 0
        here = pl.ds(pl.multiple_of(s * seq, seq), seq)

        def store(h, value):
            mixed[here, h * DH:(h + 1) * DH] = value

        attend_set(heads, vocab, ids_ref[s], inv_ref[s], masked, table, store)

    for n, pair in enumerate(pairs):
        if n + 1 < len(pairs):
            move(pairs[n + 1], last - 1)
        for c in pair:
            gather.finish(c, last)
            scatter.advance(c)
    for step in range(chunks, scatter.steps()):
        scatter.advance(step)


def run_whole(partial, w_out, ids, inv, valid, row_count, part_count, heads, vocab):
    rows, cols = partial.shape
    sets, seq = ids.shape
    depth, own = w_out.shape
    piece = 128
    chunks = own // piece
    features = own * row_count // part_count
    levels = tuple(range(row_count.bit_length() - 1))
    count = part_count.bit_length() - 1
    half, width = part_count // 2, features // chunks
    chunk = 640
    pieces = cols // chunk
    flat = sets * seq
    vmem = pl.BlockSpec(memory_space=pltpu.VMEM)
    dma = pltpu.SemaphoreType.DMA
    return pl.pallas_call(
        functools.partial(whole_kernel, levels, count, heads, vocab, chunk),
        out_shape=jax.ShapeDtypeStruct((flat, features), jnp.bfloat16),
        in_specs=[vmem] * 5,
        out_specs=vmem,
        scratch_shapes=[
            pltpu.VMEM((rows, cols), jnp.bfloat16),
            pltpu.VMEM((rows, cols), jnp.bfloat16),
            pltpu.VMEM((rows, cols), jnp.bfloat16),
            pltpu.VMEM((chunks, row_count, depth, piece), jnp.bfloat16),
            pltpu.VMEM((flat, heads * DH), jnp.bfloat16),
            pltpu.VMEM((chunks, half, flat, width), jnp.bfloat16),
            pltpu.VMEM((chunks, 2 * half - 1, flat, width), jnp.bfloat16),
            dma((2, pieces, 2 * len(levels))),
            dma((2, chunks, row_count - 1)),
            dma((2, chunks, count)),
        ],
        compiler_params=pltpu.CompilerParams(
            collective_id=2, has_side_effects=True, vmem_limit_bytes=60 * 1024 * 1024
        ),
        cost_estimate=pl.CostEstimate(
            flops=2 * flat * depth * own * row_count, bytes_accessed=2 * flat * depth * 20,
            transcendentals=0,
        ),
    )(partial, w_out, ids[..., None], inv[..., None], valid[:, None, :])


def on_device(
    row_count, part_count, token_ids, set_lengths, live_counts, embed_table, position_table, norm_gain,
    w_query, w_key, w_value, w_out,
):
    sets, seq = token_ids.shape
    vocab, d = embed_table.shape
    me, part = lax.axis_index("row"), lax.axis_index("mp")
    depth, width = w_query.shape
    heads = width // DH

    rows = jnp.concatenate([
        lax.dynamic_slice_in_dim(embed_table, me * depth, depth, 1),
        lax.dynamic_slice_in_dim(position_table, me * depth, depth, 1),
    ], axis=0).astype(jnp.float32)
    rows = (rows * lax.dynamic_slice_in_dim(norm_gain, me * depth, depth)).astype(jnp.bfloat16)
    short = -rows.shape[0] % (16 * row_count)
    if short:
        rows = jnp.pad(rows, ((0, short), (0, 0)))
    partial = jnp.concatenate([
        jnp.dot(rows, w, preferred_element_type=jnp.float32).astype(jnp.bfloat16)
        for w in (w_query, w_key, w_value)
    ], axis=1)

    pick = (token_ids.reshape(-1, 1) == jnp.arange(vocab)[None]).astype(jnp.bfloat16)
    picked = jnp.dot(pick, embed_table, preferred_element_type=jnp.float32)
    stored = (
        picked.reshape(sets, seq, d) + position_table.astype(jnp.float32)[None]
    ).astype(jnp.bfloat16)
    widened = stored.astype(jnp.float32)
    inv = lax.rsqrt(jnp.mean(widened * widened, axis=-1) + 1e-05)

    live = jnp.arange(sets) < live_counts[me]
    valid = jnp.arange(seq)[None, :] < set_lengths[:, None]
    aligned = w_out.shape[1] % 128 == 0 and partial.shape[1] % 640 == 0
    if aligned:
        summed = run_whole(
            partial, w_out, token_ids, inv, valid.astype(jnp.int32), row_count, part_count,
            heads, vocab,
        )
    else:
        table = sum_over_rows(partial, row_count)
        out_full = lax.all_gather(w_out, "row", axis=1, tiled=True)
        mixed = attend(
            token_ids, set_lengths, live.astype(jnp.int32), inv, table, heads, vocab
        )
        summed = project_out(mixed, out_full, part_count)
    summed = summed.astype(jnp.float32)
    features = summed.shape[1]
    residual = lax.dynamic_slice_in_dim(
        stored.reshape(sets * seq, d), part * features, features, 1
    ).astype(jnp.float32)
    keep = (live[:, None] & valid).reshape(-1, 1)
    output = jnp.where(keep, residual + summed, 0.0).astype(jnp.bfloat16)
    return output.reshape(sets, seq, features)


def solution(mesh):
    in_specs = (
        P("row", None), P("row"), P(), P(), P(), P(),
        P("row", "mp"), P("row", "mp"), P("row", "mp"), P("mp", "row"),
    )
    return jax.shard_map(
        functools.partial(on_device, mesh.shape["row"], mesh.shape["mp"]), mesh=mesh, in_specs=in_specs, out_specs=P("row", None, "mp"), check_vma=False
    )
```

```python
import functools
import jax
import jax.numpy as jnp
from jax import lax
from jax.experimental import pallas as pl
from jax.experimental.pallas import tpu as pltpu
from jax.sharding import PartitionSpec as P

DH = 128


def attend_set(heads, vocab, ids, inv, masked, table_ref, store):
    seq = ids.shape[0]
    width = heads * DH
    cols = lax.broadcasted_iota(jnp.int32, (seq, vocab + seq), 1)
    rows = lax.broadcasted_iota(jnp.int32, (seq, vocab + seq), 0)
    pick = jnp.where((cols == ids) | (cols == rows + vocab), 1.0, 0.0).astype(jnp.bfloat16)
    pieces = {}
    for part in range(3):
        at = 0
        while at < width:
            step = min(2 * DH, width - at)
            got = jnp.dot(
                pick, table_ref[:vocab + seq, part * width + at:part * width + at + step],
                preferred_element_type=jnp.float32,
            )
            got = (got * inv).astype(jnp.bfloat16)
            for k in range(step // DH):
                pieces[part, at // DH + k] = got[:, k * DH:(k + 1) * DH]
            at += step
    for h in range(heads):
        q, k, v = pieces[0, h], pieces[1, h], pieces[2, h]
        scores = lax.dot_general(
            q, k, (((1,), (1,)), ((), ())), preferred_element_type=jnp.float32
        ) * DH ** (-0.5)
        scores = jnp.where(masked, -1e30, scores)
        expo = jnp.exp(scores - jnp.max(scores, axis=-1, keepdims=True))
        weights = (expo / jnp.sum(expo, axis=-1, keepdims=True)).astype(jnp.bfloat16)
        mixed = jnp.dot(weights, v, preferred_element_type=jnp.float32)
        store(h, mixed.astype(jnp.bfloat16))


def attend_kernel(heads, vocab, lengths_ref, live_ref, ids_ref, inv_ref, table_ref, out_ref):
    s = pl.program_id(0)
    seq = out_ref.shape[0]
    width = heads * DH
    length = lengths_ref[s]

    @pl.when(live_ref[s] == 0)
    def _():
        out_ref[...] = jnp.zeros_like(out_ref)

    @pl.when(live_ref[s] != 0)
    def _():
        masked = lax.broadcasted_iota(jnp.int32, (seq, seq), 1) >= length

        def store(h, value):
            out_ref[:, h * DH:(h + 1) * DH] = value

        attend_set(
            heads, vocab, ids_ref[...].reshape(seq, 1), inv_ref[...].reshape(seq, 1), masked,
            table_ref, store,
        )


def attend(ids, lengths, live, inv, table, heads, vocab):
    sets, seq = ids.shape
    width = heads * DH
    grid_spec = pltpu.PrefetchScalarGridSpec(
        num_scalar_prefetch=2,
        grid=(sets,),
        in_specs=[
            pl.BlockSpec((None, seq, 1), lambda s, *_: (s, 0, 0)),
            pl.BlockSpec((None, seq, 1), lambda s, *_: (s, 0, 0)),
            pl.BlockSpec(table.shape, lambda s, *_: (0, 0)),
        ],
        out_specs=pl.BlockSpec((seq, width), lambda s, *_: (s, 0)),
    )
    return pl.pallas_call(
        functools.partial(attend_kernel, heads, vocab),
        out_shape=jax.ShapeDtypeStruct((sets * seq, width), jnp.bfloat16),
        grid_spec=grid_spec,
        compiler_params=pltpu.CompilerParams(vmem_limit_bytes=40 * 1024 * 1024),
        cost_estimate=pl.CostEstimate(
            flops=2 * sets * seq * (vocab + seq) * 3 * width,
            bytes_accessed=2 * (vocab + seq) * 3 * width,
            transcendentals=sets * seq * seq * heads,
        ),
    )(lengths, live, ids[..., None], inv[..., None], table)


def bit_of(index, bit):
    return lax.rem(index // (1 << bit), 2)


def flip(me, bit):
    return me + (1 - 2 * (lax.rem(me // (1 << bit), 2))) * (1 << bit)


class RowSum:
    def __init__(self, me, levels, chunk, part, out, land, acc, send_sem, recv_sem):
        self.me, self.levels, self.chunk = me, levels, chunk
        self.part, self.out, self.land, self.acc = part, out, land, acc
        self.send_sem, self.recv_sem = send_sem, recv_sem
        self.rows, cols = part.shape
        self.chunks, self.count = cols // chunk, len(levels)
        self.flying = {}

    def order(self, c):
        levels = self.levels
        return levels if c % 2 == 0 or c > 4 else (levels[1], levels[0]) + levels[2:]

    def span(self, c, level):
        low, size = 0, self.rows
        for bit in self.order(c)[:level]:
            size = size // 2
            low = low + bit_of(self.me, bit) * size
        return low, size

    def start(self, c, stage):
        at = pl.ds(c * self.chunk, self.chunk)
        if stage < self.count:
            level, bit = stage, self.order(c)[stage]
            low, size = self.span(c, level)
            half = size // 2
            theirs = low + (1 - bit_of(self.me, bit)) * half
            if level:
                theirs = theirs - self.span(c, 1)[0]
            held = self.acc if level else self.part
            src = held.at[pl.ds(pl.multiple_of(theirs, 16), half), at]
            dst = self.land.at[pl.ds(self.rows - size, half), at]
        else:
            level = 2 * self.count - 1 - stage
            bit = self.order(c)[level]
            low, size = self.span(c, level + 1)
            src = self.out.at[pl.ds(pl.multiple_of(low, 16), size), at]
            dst = src
        copy = pltpu.make_async_remote_copy(
            src_ref=src, dst_ref=dst,
            send_sem=self.send_sem.at[c, stage], recv_sem=self.recv_sem.at[c, stage],
            device_id={"row": flip(self.me, bit)}, device_id_type=pl.DeviceIdType.MESH,
        )
        copy.start()
        self.flying[c, stage] = copy

    def finish(self, c, stage):
        self.flying[c, stage].wait()
        if stage < self.count:
            at = pl.ds(c * self.chunk, self.chunk)
            low, size = self.span(c, stage + 1)
            here = pl.ds(pl.multiple_of(low, 16), size)
            kept = pl.ds(pl.multiple_of(low - self.span(c, 1)[0], 16), size)
            mine = self.acc[kept, at] if stage else self.part[here, at]
            mine = mine.astype(jnp.float32)
            got = self.land[pl.ds(self.rows - 2 * size, size), at].astype(jnp.float32)
            total = (mine + got).astype(jnp.bfloat16)
            if stage == self.count - 1:
                self.out[here, at] = total
            else:
                self.acc[kept, at] = total

    def run(self, beside=None):
        stages, ahead = 2 * self.count, 4
        for c in range(min(ahead, self.chunks)):
            self.start(c, 0)
        for step in range(stages + (self.chunks - 1) // 2):
            if beside is not None:
                beside(step)
            for c in range(self.chunks):
                stage = step - c // 2
                if 0 <= stage < stages:
                    self.finish(c, stage)
                    if stage + 1 < stages:
                        self.start(c, stage + 1)
                    if stage == 0 and c + ahead < self.chunks:
                        self.start(c + ahead, 0)


def greet(me, count, part, part_count):
    barrier = pltpu.get_barrier_semaphore()
    for bit in range(count):
        pl.semaphore_signal(
            barrier, inc=1, device_id={"row": flip(me, bit)}, device_id_type=pl.DeviceIdType.MESH
        )
    for bit in range(part_count):
        pl.semaphore_signal(
            barrier, inc=1, device_id={"mp": flip(part, bit)}, device_id_type=pl.DeviceIdType.MESH
        )
    pl.semaphore_wait(barrier, count + part_count)


def sum_kernel(levels, chunk, part_ref, out_ref, land, acc, send_sem, recv_sem):
    me = lax.axis_index("row")
    greet(me, len(levels), 0, 0)
    RowSum(me, levels, chunk, part_ref, out_ref, land, acc, send_sem, recv_sem).run()


def sum_over_rows(partial, row_count):
    rows, cols = partial.shape
    levels = tuple(range(row_count.bit_length() - 1))
    count = len(levels)
    chunk = 640 if cols % 640 == 0 else 128
    chunks = cols // chunk
    whole = pl.BlockSpec(memory_space=pltpu.VMEM)
    return pl.pallas_call(
        functools.partial(sum_kernel, levels, chunk),
        out_shape=jax.ShapeDtypeStruct((rows, cols), jnp.bfloat16),
        in_specs=[whole],
        out_specs=whole,
        scratch_shapes=[
            pltpu.VMEM((rows, cols), jnp.bfloat16),
            pltpu.VMEM((rows // 2, cols), jnp.bfloat16),
            pltpu.SemaphoreType.DMA((chunks, 2 * count)),
            pltpu.SemaphoreType.DMA((chunks, 2 * count)),
        ],
        compiler_params=pltpu.CompilerParams(
            collective_id=0, has_side_effects=True, vmem_limit_bytes=40 * 1024 * 1024
        ),
        cost_estimate=pl.CostEstimate(
            flops=2 * rows * cols, bytes_accessed=200 * rows * cols, transcendentals=0
        ),
    )(partial)


class Scatter:
    def __init__(self, part, count, mixed, weight, out, buf, land, send_sem, recv_sem):
        self.part, self.count = part, count
        self.mixed, self.weight, self.out = mixed, weight, out
        self.buf, self.land = buf, land
        self.send_sem, self.recv_sem = send_sem, recv_sem
        self.chunks, self.half, self.rows, self.width = buf.shape
        self.flying = {}

    def columns(self, c, block):
        at = pl.multiple_of(block * self.chunks * self.width + c * self.width, 128)
        return self.weight[:, pl.ds(at, self.width)]

    def store(self, c, here, value):
        self.out[here, pl.ds(c * self.width, self.width)] = value.astype(jnp.bfloat16)

    def product(self, c, mine, finish):
        tile = min(256, self.rows)
        first = bit_of(self.part, 0)
        first = first if mine else 1 - first
        for p in range(self.half):
            block = first
            for i in range(1, self.count):
                block = block + (1 << i) * ((p >> (self.count - 1 - i)) & 1)
            load = functools.partial(self.columns, c, block)

            @pl.loop(0, self.rows // tile)
            def _(t):
                here = pl.ds(pl.multiple_of(t * tile, tile), tile)
                got = jnp.dot(
                    self.mixed[here, :], load(),
                    preferred_element_type=jnp.float32,
                )
                if mine:
                    got = got + self.land[c, p, here, :].astype(jnp.float32)
                finish(c, p, here, got.astype(jnp.bfloat16))

    def kept(self, level):
        low, size = 0, self.half
        for bit in range(1, level + 1):
            size = size // 2
            low = low + bit_of(self.part, bit) * size
        return low, size

    def start(self, c, level):
        if level == 0:
            def store(c, p, here, value):
                self.buf[c, p, here, :] = value
            self.product(c, False, store)
            src, dst = self.buf.at[c], self.land.at[c, pl.ds(0, self.half)]
        else:
            low, size = self.kept(level - 1)
            size = size // 2
            theirs = low + (1 - bit_of(self.part, level)) * size
            src = self.buf.at[c, pl.ds(theirs, size)]
            dst = self.land.at[c, pl.ds(2 * self.half - 2 * size, size)]
        copy = pltpu.make_async_remote_copy(
            src_ref=src, dst_ref=dst,
            send_sem=self.send_sem.at[c, level], recv_sem=self.recv_sem.at[c, level],
            device_id={"mp": flip(self.part, level)}, device_id_type=pl.DeviceIdType.MESH,
        )
        copy.start()
        self.flying[c, level] = copy

    def finish(self, c, level):
        self.flying[c, level].wait()
        last = level == self.count - 1
        if level == 0:
            def store(c, p, here, value):
                if last:
                    self.store(c, here, value)
                else:
                    self.buf[c, p, here, :] = value
            self.product(c, True, store)
        else:
            low, size = self.kept(level)
            tile = min(256, self.rows)
            for k in range(size):
                @pl.loop(0, self.rows // tile)
                def _(t):
                    here = pl.ds(pl.multiple_of(t * tile, tile), tile)
                    got = self.land[c, 2 * self.half - 2 * size + k, here, :].astype(jnp.float32)
                    value = self.buf[c, low + k, here, :].astype(jnp.float32) + got
                    if last:
                        self.store(c, here, value)
                    else:
                        self.buf[c, low + k, here, :] = value.astype(jnp.bfloat16)

    def advance(self, step):
        if step < self.chunks:
            self.start(step, 0)
        for level in range(self.count):
            c = step - 1 - level
            if 0 <= c < self.chunks:
                self.finish(c, level)
                if level + 1 < self.count:
                    self.start(c, level + 1)

    def steps(self):
        return self.chunks + self.count


def scatter_kernel(count, mixed_ref, weight_ref, out_ref, buf, land, send_sem, recv_sem):
    part = lax.axis_index("mp")
    barrier = pltpu.get_barrier_semaphore()
    for bit in range(count):
        pl.semaphore_signal(
            barrier, inc=1, device_id={"mp": flip(part, bit)}, device_id_type=pl.DeviceIdType.MESH
        )
    pl.semaphore_wait(barrier, count)
    work = Scatter(part, count, mixed_ref, weight_ref, out_ref, buf, land, send_sem, recv_sem)
    for step in range(work.steps()):
        work.advance(step)


def project_out(mixed, weight, part_count):
    rows = mixed.shape[0]
    features = weight.shape[1] // part_count
    count = part_count.bit_length() - 1
    chunks = 5 if features % 640 == 0 else 1
    width = features // chunks
    half = part_count // 2
    whole = pl.BlockSpec(memory_space=pltpu.VMEM)
    return pl.pallas_call(
        functools.partial(scatter_kernel, count),
        out_shape=jax.ShapeDtypeStruct((rows, features), jnp.bfloat16),
        in_specs=[whole, whole],
        out_specs=whole,
        scratch_shapes=[
            pltpu.VMEM((chunks, half, rows, width), jnp.bfloat16),
            pltpu.VMEM((chunks, 2 * half - 1, rows, width), jnp.bfloat16),
            pltpu.SemaphoreType.DMA((chunks, count)),
            pltpu.SemaphoreType.DMA((chunks, count)),
        ],
        compiler_params=pltpu.CompilerParams(
            collective_id=1, has_side_effects=True, vmem_limit_bytes=56 * 1024 * 1024
        ),
        cost_estimate=pl.CostEstimate(
            flops=2 * rows * mixed.shape[1] * weight.shape[1],
            bytes_accessed=2 * weight.size, transcendentals=0,
        ),
    )(mixed, weight)


class Gather:
    def __init__(self, me, levels, held, send_sem, recv_sem):
        self.me, self.levels, self.held = me, levels, held
        self.send_sem, self.recv_sem = send_sem, recv_sem
        self.flying = {}

    def order(self, c):
        order = tuple(reversed(self.levels))
        return order if c != 1 else order[:-2] + (order[-1], order[-2])

    def start(self, c, level):
        order = self.order(c)
        to = flip(self.me, order[level])
        for i in range(1 << level):
            block = self.me
            for k in range(level):
                if (i >> k) & 1:
                    block = flip(block, order[k])
            slot = (1 << level) - 1 + i
            copy = pltpu.make_async_remote_copy(
                src_ref=self.held.at[c, block], dst_ref=self.held.at[c, block],
                send_sem=self.send_sem.at[c, slot], recv_sem=self.recv_sem.at[c, slot],
                device_id={"row": to}, device_id_type=pl.DeviceIdType.MESH,
            )
            copy.start()
            self.flying[c, slot] = copy

    def finish(self, c, level):
        for i in range(1 << level):
            self.flying[c, (1 << level) - 1 + i].wait()


class BlockScatter(Scatter):
    def columns(self, c, block):
        per = self.width // self.weight.shape[-1]
        return jnp.concatenate([self.weight[c, block * per + q] for q in range(per)], axis=1)

    def store(self, c, here, value):
        piece = self.weight.shape[-1]
        for q in range(self.width // piece):
            at = q * self.chunks * piece + c * piece
            full = self.out[here, pl.ds(at, piece)].astype(jnp.float32)
            full = full + value[:, q * piece:(q + 1) * piece]
            full = jnp.where(self.keep[here, :] != 0, full, 0.0)
            self.out[here, pl.ds(at, piece)] = full.astype(jnp.bfloat16)


def whole_kernel(
    levels, count, heads, vocab, chunk, part_ref, w_ref, ids_ref, valid_ref, keep_ref,
    embed_ref, position_ref, out_ref, table, land, acc, inv, held, mixed, buf, land_out, row_sems, held_sems, out_sems,
):
    me, part = lax.axis_index("row"), lax.axis_index("mp")
    sets, seq, _ = ids_ref.shape
    chunks, _, _, piece = held.shape
    greet(me, len(levels), part, count)
    for c in range(chunks):
        held[c, me] = w_ref[:, c * piece:(c + 1) * piece]
    gather = Gather(me, levels, held, held_sems.at[0], held_sems.at[1])
    total = RowSum(me, levels, chunk, part_ref, table, land, acc, row_sems.at[0], row_sems.at[1])
    scatter = BlockScatter(part, count, mixed, held, out_ref, buf, land_out, out_sems.at[0], out_sems.at[1])
    scatter.keep = keep_ref
    last = len(levels) - 1
    d, features = embed_ref.shape[1], out_ref.shape[1]

    def prepare(s):
        columns = lax.broadcasted_iota(jnp.int32, (seq, vocab), 1)
        pick = jnp.where(columns == ids_ref[s], 1.0, 0.0).astype(jnp.bfloat16)

        def stored(at):
            got = jnp.dot(pick, embed_ref[:, at], preferred_element_type=jnp.float32)
            return (got + position_ref[:, at].astype(jnp.float32)).astype(jnp.bfloat16)

        squares = jnp.zeros((seq, 1), jnp.float32)
        for k in range(0, d, 512):
            wide = stored(slice(k, min(k + 512, d))).astype(jnp.float32)
            squares = squares + jnp.sum(wide * wide, axis=1, keepdims=True)
        inv[s] = lax.rsqrt(squares / d + 1e-05)
        here = pl.ds(pl.multiple_of(s * seq, seq), seq)
        for k in range(0, features, 128):
            at = pl.ds(pl.multiple_of(part * features + k, 128), 128)
            out_ref[here, k:k + 128] = stored(at)

    def beside(step):
        if step == 0:
            for c in range(chunks):
                gather.start(c, 0)
            pl.loop(0, sets)(prepare)
        for c in range(chunks):
            if step == (len(levels) + 1 if c < 2 else 2 * len(levels)):
                for level in range(last - 1):
                    gather.finish(c, level)
                    gather.start(c, level + 1)

    total.run(beside)
    pairs = [tuple(range(c, min(c + 2, chunks))) for c in range(0, chunks, 2)]

    def move(pair, level):
        for c in pair:
            gather.finish(c, level)
            gather.start(c, level + 1)

    move(pairs[0], last - 1)

    @pl.loop(0, sets)
    def _(s):
        masked = jnp.broadcast_to(valid_ref[s], (seq, seq)) == 0
        here = pl.ds(pl.multiple_of(s * seq, seq), seq)

        def store(h, value):
            mixed[here, h * DH:(h + 1) * DH] = value

        attend_set(heads, vocab, ids_ref[s], inv[s], masked, table, store)

    for n, pair in enumerate(pairs):
        if n + 1 < len(pairs):
            move(pairs[n + 1], last - 1)
        for c in pair:
            gather.finish(c, last)
            scatter.advance(c)
    for step in range(chunks, scatter.steps()):
        scatter.advance(step)


def run_whole(partial, w_out, ids, valid, keep, embed, position, row_count, part_count, heads):
    rows, cols = partial.shape
    sets, seq = ids.shape
    vocab = embed.shape[0]
    depth, own = w_out.shape
    piece = 128
    chunks = own // piece
    features = own * row_count // part_count
    levels = tuple(range(row_count.bit_length() - 1))
    count = part_count.bit_length() - 1
    half, width = part_count // 2, features // chunks
    chunk = 640
    pieces = cols // chunk
    flat = sets * seq
    vmem = pl.BlockSpec(memory_space=pltpu.VMEM)
    dma = pltpu.SemaphoreType.DMA
    return pl.pallas_call(
        functools.partial(whole_kernel, levels, count, heads, vocab, chunk),
        out_shape=jax.ShapeDtypeStruct((flat, features), jnp.bfloat16),
        in_specs=[vmem] * 7,
        out_specs=vmem,
        scratch_shapes=[
            pltpu.VMEM((rows, cols), jnp.bfloat16),
            pltpu.VMEM((rows, cols), jnp.bfloat16),
            pltpu.VMEM((rows // 2, cols), jnp.bfloat16),
            pltpu.VMEM((sets, seq, 1), jnp.float32),
            pltpu.VMEM((chunks, row_count, depth, piece), jnp.bfloat16),
            pltpu.VMEM((flat, heads * DH), jnp.bfloat16),
            pltpu.VMEM((chunks, half, flat, width), jnp.bfloat16),
            pltpu.VMEM((chunks, 2 * half - 1, flat, width), jnp.bfloat16),
            dma((2, pieces, 2 * len(levels))),
            dma((2, chunks, row_count - 1)),
            dma((2, chunks, count)),
        ],
        compiler_params=pltpu.CompilerParams(
            collective_id=2, has_side_effects=True, vmem_limit_bytes=60 * 1024 * 1024
        ),
        cost_estimate=pl.CostEstimate(
            flops=2 * flat * depth * own * row_count, bytes_accessed=2 * flat * depth * 20,
            transcendentals=0,
        ),
    )(partial, w_out, ids[..., None], valid[:, None, :], keep, embed, position)


def on_device(
    row_count, part_count, token_ids, set_lengths, live_counts, embed_table, position_table, norm_gain,
    w_query, w_key, w_value, w_out,
):
    sets, seq = token_ids.shape
    vocab, d = embed_table.shape
    me, part = lax.axis_index("row"), lax.axis_index("mp")
    depth, width = w_query.shape
    heads = width // DH

    rows = jnp.concatenate([
        lax.dynamic_slice_in_dim(embed_table, me * depth, depth, 1),
        lax.dynamic_slice_in_dim(position_table, me * depth, depth, 1),
    ], axis=0).astype(jnp.float32)
    rows = (rows * lax.dynamic_slice_in_dim(norm_gain, me * depth, depth)).astype(jnp.bfloat16)
    short = -rows.shape[0] % (16 * row_count)
    if short:
        rows = jnp.pad(rows, ((0, short), (0, 0)))
    partial = jnp.concatenate([
        jnp.dot(rows, w, preferred_element_type=jnp.float32).astype(jnp.bfloat16)
        for w in (w_query, w_key, w_value)
    ], axis=1)

    live = jnp.arange(sets) < live_counts[me]
    valid = jnp.arange(seq)[None, :] < set_lengths[:, None]
    keep = (live[:, None] & valid).reshape(-1, 1)
    aligned = (
        w_out.shape[1] % 128 == 0 and partial.shape[1] % 640 == 0 and row_count == 8
        and part_count >= 4
    )
    if aligned:
        return run_whole(
            partial, w_out, token_ids, valid.astype(jnp.int32), keep.astype(jnp.int32),
            embed_table, position_table, row_count, part_count, heads,
        ).reshape(sets, seq, -1)

    pick = (token_ids.reshape(-1, 1) == jnp.arange(vocab)[None]).astype(jnp.bfloat16)
    picked = jnp.dot(pick, embed_table, preferred_element_type=jnp.float32)
    stored = (
        picked.reshape(sets, seq, d) + position_table.astype(jnp.float32)[None]
    ).astype(jnp.bfloat16)
    widened = stored.astype(jnp.float32)
    inv = lax.rsqrt(jnp.mean(widened * widened, axis=-1) + 1e-05)
    table = sum_over_rows(partial, row_count)
    out_full = lax.all_gather(w_out, "row", axis=1, tiled=True)
    mixed = attend(token_ids, set_lengths, live.astype(jnp.int32), inv, table, heads, vocab)
    summed = project_out(mixed, out_full, part_count).astype(jnp.float32)
    features = summed.shape[1]
    residual = lax.dynamic_slice_in_dim(
        stored.reshape(sets * seq, d), part * features, features, 1
    ).astype(jnp.float32)
    output = jnp.where(keep, residual + summed, 0.0).astype(jnp.bfloat16)
    return output.reshape(sets, seq, features)


def solution(mesh):
    in_specs = (
        P("row", None), P("row"), P(), P(), P(), P(),
        P("row", "mp"), P("row", "mp"), P("row", "mp"), P("mp", "row"),
    )
    return jax.shard_map(
        functools.partial(on_device, mesh.shape["row"], mesh.shape["mp"]), mesh=mesh, in_specs=in_specs, out_specs=P("row", None, "mp"), check_vma=False
    )
```
